1024 devices in a mesh: dp: 2 (over core), expert: 64 (over y, x), tensor: 8 (over z).
Axes of the slice: x: 8, y: 8, z: 8, core: 2. Of those that a mesh axis runs over, the one named last changes fastest.
Arguments:
- latent: bfloat16 [16384, 1024], P(('dp', 'expert')), may hold values from -6 to 6
- grad_out: bfloat16 [16384, 1024], P(('dp', 'expert')), may hold values from -6 to 6
- expert_weights: bfloat16 [2, 128, 1024, 2048], P(None, 'expert', None, 'tensor'), may hold values from -0.1875 to 0.1875
- expert_ids: int32 [16384, 8], P(('dp', 'expert')), may hold values from 0 to 127, as said below
- slot_index: int32 [16384, 8], P(('dp', 'expert')), may hold values from 0 to 7, as said below
- kept: int32 [16384, 8], P(('dp', 'expert')), may hold values from 0 to 1
- gate_weights: float32 [16384, 8], P(('dp', 'expert')), may hold values from 0.1 to 1
Outputs:
- mixed: bfloat16 [16384, 1024], P(('dp', 'expert'), 'tensor')
- latent_grad: bfloat16 [16384, 1024], P(('dp', 'expert'), 'tensor')
- weight_grads: float32 [2, 128, 1024, 2048], P(None, 'expert', 'dp', 'tensor')
The draws below stay inside these ranges and needn't reach their ends.
Inputs may be any that keep to these rules, and one draw needn't show every extreme that they name: `expert_ids`: each token names 8 different experts. `slot_index`: kept pairs of one block of 128 tokens and one expert have distinct slots; slot 7 is used in every block, and one expert has all its 8 slots used in every block of one dp index.
All inputs are finite; a program needn't handle non-finite values.
Results may differ from the reference program's by a relative error of at most 0.02.
Values may be sent and summed in bfloat16 or wider, within the bound.
A program may use at most 64 MiB of HBM per device.

```python
import jax
import jax.numpy as jnp
from jax import lax

LATENT = 1024
FF = 2048
TOPK = 8
EXPERTS = 128
TOK_DEV = 128
CAP = 8
TOKENS = 16384
N_DP = 2
N_EXPERT = 64
N_TENSOR = 8


def routing(key):
    blocks = TOKENS // TOK_DEV
    rows_dp = TOKENS // (TOK_DEV * N_EXPERT)
    base = jax.random.randint(jax.random.fold_in(key, 11), (TOKENS, EXPERTS), 0, 4096)
    raw_pop = jax.random.randint(jax.random.fold_in(key, 12), (EXPERTS,), 0, 64)
    popular = raw_pop * 8
    hot = jax.random.randint(jax.random.fold_in(key, 13), (rows_dp,), 0, EXPERTS)
    positions = jnp.arange(TOKENS, dtype=jnp.int32)
    hot_row = hot[positions // (TOK_DEV * N_EXPERT)]
    columns = jnp.arange(EXPERTS, dtype=jnp.int32)
    forced = jnp.where((positions % TOK_DEV < CAP)[:, None] & (columns[None, :] == hot_row[:, None]), 16384, 0)
    score = (base + popular[None, :] + forced) * EXPERTS + columns[None, :]
    _, ids = lax.top_k(score, TOPK)
    ids = ids.astype(jnp.int32)
    onehot = (ids[..., None] == columns).astype(jnp.int32).reshape(blocks, TOK_DEV * TOPK, EXPERTS)
    before = jnp.cumsum(onehot, axis=1) - onehot
    rank = jnp.sum(before * onehot, axis=-1).reshape(TOKENS, TOPK)
    keep = (rank < CAP).astype(jnp.int32)
    slots = jnp.minimum(rank, CAP - 1).astype(jnp.int32)
    return (ids, slots, keep)


def draw_expert_ids(key, part):
    ids, slots, keep = routing(key)
    return ids


def draw_slot_index(key, part):
    ids, slots, keep = routing(key)
    return slots


def draw_kept(key, part):
    ids, slots, keep = routing(key)
    return keep


def steps_of(own_key, extent, split, smallest, largest):
    gain, own = 1.0, jax.random.fold_in(own_key, 6)
    for dim, parts in split:
        steps = jnp.exp(jax.random.uniform(jax.random.fold_in(own, dim), (parts,), jnp.float32, smallest / len(split), largest / len(split)))
        gain = gain * jnp.repeat(steps, extent[dim] // parts).reshape([-1 if axis == dim else 1 for axis in range(len(extent))])
    return gain


def normal_values(own_key, shape, scale, reach, shards=(), kind=jnp.bfloat16):
    drawn = scale * jax.random.normal(own_key, shape, jnp.float32)
    if shards:
        drawn = drawn * steps_of(own_key, shape, shards, -0.22, 0.18)
    return jnp.clip(drawn, -reach, reach).astype(kind)


def setup_inputs(seed: int = 0) -> dict:
    splits = jax.random.split(jax.random.key(seed), 8)
    latent = normal_values(splits[0], (TOKENS, LATENT), 1.0, 6.0, ((0, 128),))
    grad_out = normal_values(splits[1], (TOKENS, LATENT), 1.0, 6.0, ((0, 128),))
    expert_weights = normal_values(splits[2], (2, EXPERTS, LATENT, FF), LATENT ** -0.5, 0.1875, ((1, 64), (3, 8)))
    expert_ids = draw_expert_ids(jax.random.fold_in(splits[7], 71), 0)
    slot_index = draw_slot_index(jax.random.fold_in(splits[7], 71), 0)
    kept = draw_kept(jax.random.fold_in(splits[7], 71), 0)
    gate_weights = jnp.clip(0.1 + 0.9 * jax.random.uniform(splits[6], (TOKENS, TOPK), jnp.float32) ** steps_of(splits[6], (TOKENS, TOPK), ((0, 128),), -0.2, 0.2), 0.1, 1.0)
    return dict(latent=latent, grad_out=grad_out, expert_weights=expert_weights, expert_ids=expert_ids, slot_index=slot_index, kept=kept, gate_weights=gate_weights)


def build(lat_rows, grad_rows, ids, slots, keep, gates):
    ntok = lat_rows.shape[0]
    dump = EXPERTS * CAP
    target = jnp.where(keep > 0, ids * CAP + slots, dump).reshape(-1).astype(jnp.int32)
    pairs = jnp.arange(ntok * TOPK, dtype=jnp.int32)
    source = jnp.full((dump + 1,), ntok * TOPK, jnp.int32).at[target].set(pairs)[:dump]
    token_of = source // TOPK
    zero_row = jnp.zeros((1, LATENT), jnp.bfloat16)
    lat_pad = jnp.concatenate([lat_rows, zero_row], 0)
    grad_pad = jnp.concatenate([grad_rows, zero_row], 0)
    gate_pad = jnp.concatenate([gates.reshape(-1), jnp.zeros((1,), jnp.float32)], 0)
    rows_in = lat_pad[token_of]
    scaled = (gate_pad[source][:, None] * grad_pad[token_of].astype(jnp.float32)).astype(jnp.bfloat16)
    return rows_in, scaled


def padded_capacity(values):
    return lax.optimization_barrier(values.astype(jnp.bfloat16)).astype(jnp.float32)


def blockwise(left, right):
    count = left.shape[0]
    width = FF // N_TENSOR
    left3 = left.reshape(count, N_TENSOR, width).astype(jnp.float32)
    right3 = right.reshape(LATENT, N_TENSOR, width).astype(jnp.float32)
    pieces = jnp.einsum("rqf,lqf->qrl", left3, right3)
    return jnp.sum(padded_capacity(pieces), axis=0).astype(jnp.bfloat16)


def reference(latent, grad_out, expert_weights, expert_ids, slot_index, kept, gate_weights):
    blocks = TOKENS // TOK_DEV
    rows_in, scaled = jax.vmap(build)(
        latent.reshape(blocks, TOK_DEV, LATENT), grad_out.reshape(blocks, TOK_DEV, LATENT),
        expert_ids.reshape(blocks, TOK_DEV, TOPK), slot_index.reshape(blocks, TOK_DEV, TOPK),
        kept.reshape(blocks, TOK_DEV, TOPK), gate_weights.reshape(blocks, TOK_DEV, TOPK))
    rows_in = jnp.transpose(rows_in.reshape(blocks, EXPERTS, CAP, LATENT), (1, 0, 2, 3))
    scaled = jnp.transpose(scaled.reshape(blocks, EXPERTS, CAP, LATENT), (1, 0, 2, 3))

    def one_expert(items):
        inputs, grads, w_up, w_down = items
        inputs2 = inputs.reshape(blocks * CAP, LATENT)
        grads2 = grads.reshape(blocks * CAP, LATENT)
        pre = jnp.dot(inputs2, w_up, preferred_element_type=jnp.float32)
        active = jnp.maximum(pre, 0.0)
        hidden = (active * active).astype(jnp.bfloat16)
        out_rows = blockwise(hidden, w_down)
        hid_grad = jnp.dot(grads2, w_down, preferred_element_type=jnp.float32)
        pre_grad = (hid_grad * 2.0 * active).astype(jnp.bfloat16)
        in_rows = blockwise(pre_grad, w_up)
        expert_input_rows = inputs2.reshape(N_DP, N_EXPERT * CAP, LATENT).astype(jnp.float32)
        output_gradient_rows = grads2.reshape(N_DP, N_EXPERT * CAP, LATENT).astype(jnp.float32)
        preactivation_gradient_rows = pre_grad.reshape(N_DP, N_EXPERT * CAP, FF).astype(jnp.float32)
        hidden_activation_rows = hidden.reshape(N_DP, N_EXPERT * CAP, FF).astype(jnp.float32)
        up_weight_gradient = jnp.sum(padded_capacity(jnp.einsum("mbp,mbo->mpo", expert_input_rows, preactivation_gradient_rows)), axis=0)
        down_weight_gradient = jnp.sum(padded_capacity(jnp.einsum("mbp,mbo->mpo", output_gradient_rows, hidden_activation_rows)), axis=0)
        return (out_rows.reshape(blocks, CAP, LATENT), in_rows.reshape(blocks, CAP, LATENT), up_weight_gradient, down_weight_gradient)

    out_all, in_all, up_all, down_all = lax.map(one_expert, (rows_in, scaled, expert_weights[0], expert_weights[1]))
    out_all = jnp.transpose(out_all, (1, 0, 2, 3)).reshape(blocks, EXPERTS * CAP, LATENT)
    in_all = jnp.transpose(in_all, (1, 0, 2, 3)).reshape(blocks, EXPERTS * CAP, LATENT)

    def combine(out_buf, in_buf, ids, slots, keep, gates):
        dump = EXPERTS * CAP
        target = jnp.where(keep > 0, ids * CAP + slots, dump).astype(jnp.int32)
        zero_row = jnp.zeros((1, LATENT), jnp.bfloat16)
        out_pad = jnp.concatenate([out_buf, zero_row], 0)
        in_pad = jnp.concatenate([in_buf, zero_row], 0)
        weight = jnp.where(keep > 0, gates, 0.0)[..., None]
        keepf = jnp.where(keep > 0, 1.0, 0.0).astype(jnp.float32)[..., None]
        mixed_rows = jnp.sum(weight * out_pad[target].astype(jnp.float32), axis=1).astype(jnp.bfloat16)
        grad_rows = jnp.sum(keepf * in_pad[target].astype(jnp.float32), axis=1).astype(jnp.bfloat16)
        return mixed_rows, grad_rows

    mixed, latent_grad = jax.vmap(combine)(
        out_all, in_all, expert_ids.reshape(blocks, TOK_DEV, TOPK), slot_index.reshape(blocks, TOK_DEV, TOPK),
        kept.reshape(blocks, TOK_DEV, TOPK), gate_weights.reshape(blocks, TOK_DEV, TOPK))
    weight_grads = jnp.stack([up_all, down_all], 0)
    return mixed.reshape(TOKENS, LATENT), latent_grad.reshape(TOKENS, LATENT), weight_grads
```

```python
import jax
import jax.numpy as jnp
from jax import lax
from jax.experimental import pallas as pl
from jax.experimental.pallas import tpu as pltpu
from jax.sharding import PartitionSpec as P

SIDE = 8
RING = 8
PARTS = 4
CAP = 8
LOCAL = 2
SLICE = 128
ROWS = 128
STEPS_Y = (0, 4, 1, 7, 2, 6, 3, 5)
MESH = pl.DeviceIdType.MESH
BF16 = jnp.bfloat16
F32 = jnp.float32


def contract(left, right, dim_left, dim_right):
    return lax.dot_general(
        left, right, (((dim_left,), (dim_right,)), ((), ())), preferred_element_type=F32
    )


def block_kernel(
    ids, slot, kept, gate, lat_hbm, grad_hbm, w_hbm,
    mixed, lat_grad, own_terms, got_terms,
    lat, grad, w, mask, gate_hi, gate_lo,
    outgoing, incoming, rows, partial, sums, back, returned, hidden, pre_grad, keep_half, send_half,
    load_sem, out_send, out_recv, gather_send, gather_recv, sum_send, sum_recv,
    back_send, back_recv, term_send, term_recv, keep_sem,
):
    dp = lax.axis_index("dp")
    chip = lax.axis_index("expert")
    z = lax.axis_index("tensor")
    y, x = lax.div(chip, SIDE), lax.rem(chip, SIDE)
    peers = SIDE * SIDE
    slots = peers * LOCAL * CAP
    above, below = lax.rem(z + 1, RING), lax.rem(z + RING - 1, RING)

    barrier = pltpu.get_barrier_semaphore()

    def greet(step, carry):
        pl.semaphore_signal(
            barrier, inc=1, device_id={"expert": lax.rem(chip + step, peers)}, device_id_type=MESH
        )
        return carry

    loads = [
        pltpu.make_async_copy(lat_hbm.at[:, pl.ds(pl.multiple_of(z * SLICE, SLICE), SLICE)], lat, load_sem.at[0]),
        pltpu.make_async_copy(grad_hbm.at[:, pl.ds(pl.multiple_of(z * SLICE, SLICE), SLICE)], grad, load_sem.at[1]),
        pltpu.make_async_copy(w_hbm, w, load_sem.at[2]),
    ]
    for load in loads:
        load.start()
    lax.fori_loop(1, peers, greet, 0)
    pl.semaphore_signal(barrier, inc=1, device_id={"tensor": above}, device_id_type=MESH)
    pl.semaphore_signal(barrier, inc=1, device_id={"tensor": below}, device_id_type=MESH)
    pl.semaphore_signal(barrier, inc=1, device_id={"dp": 1 - dp}, device_id_type=MESH)

    target = jnp.where(kept[...] > 0, ids[...] * CAP + slot[...], slots)
    gates = gate[...]
    loads[0].wait()
    loads[1].wait()

    def build(step, carry):
        first = pl.multiple_of(step * 128, 128)
        slot_of = first + lax.broadcasted_iota(jnp.int32, (128, 128), 0)
        placed = jnp.zeros((128, 128), F32)
        weight = jnp.zeros((128, 128), F32)
        for k in range(ids.shape[0]):
            same = target[k : k + 1, :] == slot_of
            placed = jnp.where(same, 1.0, placed)
            weight = jnp.where(same, gates[k : k + 1, :], weight)
        hi = weight.astype(BF16)
        here = pl.ds(first, 128)
        mask[here, :] = placed.astype(BF16)
        gate_hi[here, :] = hi
        gate_lo[here, :] = (weight - hi.astype(F32)).astype(BF16)
        onehot = placed.astype(BF16)
        scale = jnp.sum(weight, axis=1, keepdims=True)
        lat_rows = contract(onehot, lat[...], 1, 0).astype(BF16)
        grad_rows = (scale * contract(onehot, grad[...], 1, 0)).astype(BF16)
        dests = pl.ds(pl.multiple_of(step * 8, 8), 8)
        outgoing[dests, 0:16, :] = lat_rows.reshape(8, 16, SLICE)
        outgoing[dests, 16:32, :] = grad_rows.reshape(8, 16, SLICE)
        return carry

    lax.fori_loop(0, slots // 128, build, 0)
    pl.semaphore_wait(barrier, peers - 1 + 3)

    def dispatch(part):
        for half in range(2):
            index = 2 * part + half
            row = lax.rem(y + STEPS_Y[index], SIDE) * SIDE

            def send(step, carry):
                dest = row + lax.rem(x + step, SIDE)
                pltpu.make_async_remote_copy(
                    src_ref=outgoing.at[dest], dst_ref=incoming.at[index * SIDE + step],
                    send_sem=out_send, recv_sem=out_recv.at[part],
                    device_id={"expert": dest}, device_id_type=MESH,
                ).start()
                return carry

            lax.fori_loop(1 if index == 0 else 0, SIDE, send, 0)

    def wait_bytes(ref, sem):
        pltpu.make_async_copy(ref, ref, sem).wait()

    def hop(part, way, step, start):
        if way == 0:
            owner, to = lax.rem(z + RING - (step - 1), RING), above
            landed = lax.rem(z + RING - step, RING)
        else:
            owner, to = lax.rem(z + step - 1, RING), below
            landed = lax.rem(z + step, RING)
        source, dest = rows.at[part, owner], rows.at[part, landed]
        if step == RING // 2:
            source, dest = rows.at[part, owner, way], rows.at[part, landed, way]
        copy = pltpu.make_async_remote_copy(
            src_ref=source, dst_ref=source if start else dest,
            send_sem=gather_send.at[part, way, step - 1],
            recv_sem=gather_recv.at[part, way, step - 1],
            device_id={"tensor": to}, device_id_type=MESH,
        )
        return copy

    def enter(part):
        first = part * 2 * SIDE
        if part == 0:
            incoming[0] = outgoing[chip]
            wait_bytes(incoming.at[pl.ds(1, 2 * SIDE - 1)], out_recv.at[part])
        else:
            wait_bytes(incoming.at[pl.ds(first, 2 * SIDE)], out_recv.at[part])
        got = incoming[pl.ds(first, 2 * SIDE)].astype(F32).reshape(2 * SIDE, 4, CAP, SLICE)
        for kind in range(2):
            for local in range(LOCAL):
                rows[part, z, kind, local] = (
                    got[:, 2 * kind + local].reshape(ROWS, SLICE).astype(BF16)
                )
        for way in range(2):
            hop(part, way, 1, True).start()

    def forward(part, step):
        for way in range(2):
            hop(part, way, step - 1, False).wait_recv()
            hop(part, way, step, True).start()

    def experts(part):
        for way in range(2):
            hop(part, way, RING // 2, False).wait_recv()

        def one(local, carry):
            got_in = jnp.concatenate([rows[part, q, 0, local] for q in range(RING)], axis=1)
            got_grad = jnp.concatenate([rows[part, q, 1, local] for q in range(RING)], axis=1)
            active = jnp.maximum(contract(got_in, w[0, local], 1, 0), 0.0)
            unit = (active * active).astype(BF16)
            unit_grad = (contract(got_grad, w[1, local], 1, 0) * 2.0 * active).astype(BF16)
            here = pl.ds(part * ROWS, ROWS)
            hidden[local, here, :] = unit
            pre_grad[local, here, :] = unit_grad
            for q in range(0, RING, 2):
                cols = pl.ds(q * SLICE, 2 * SLICE)
                out_cols = contract(unit, w[1, local, cols, :], 1, 1).astype(BF16)
                in_cols = contract(unit_grad, w[0, local, cols, :], 1, 1).astype(BF16)
                for side in range(2):
                    span = slice(side * SLICE, (side + 1) * SLICE)
                    partial[part, q + side, 0, local] = out_cols[:, span]
                    partial[part, q + side, 1, local] = in_cols[:, span]
            return carry

        lax.fori_loop(0, LOCAL, one, 0)

    def sum_hop(part, way, step):
        ahead = RING // 2 + 1 - step
        owner = lax.rem(z + ahead, RING) if way == 0 else lax.rem(z + RING - ahead, RING)
        source, dest = partial.at[part, owner], sums.at[part, way, step - 1]
        if step == 1:
            source, dest = partial.at[part, owner, way], sums.at[part, way, 0, way]
        copy = pltpu.make_async_remote_copy(
            src_ref=source, dst_ref=dest,
            send_sem=sum_send.at[part, way, step - 1],
            recv_sem=sum_recv.at[part, way, step - 1],
            device_id={"tensor": above if way == 0 else below}, device_id_type=MESH,
        )
        return owner, copy

    def add(part, step):
        for way in range(2):
            owner, copy = sum_hop(part, way, step)
            if step > 1:
                sum_hop(part, way, step - 1)[1].wait_recv()
                for kind in (range(2) if step > 2 else (way,)):
                    for local in range(LOCAL):
                        partial[part, owner, kind, local] = (
                            partial[part, owner, kind, local].astype(F32)
                            + sums[part, way, step - 2, kind, local].astype(F32)
                        ).astype(BF16)
            copy.start()

    def give_back(part):
        for way in range(2):
            sum_hop(part, way, RING // 2)[1].wait_recv()
        pieces = []
        for kind in range(2):
            for local in range(LOCAL):
                total = (
                    partial[part, z, kind, local].astype(F32)
                    + sums[part, 0, RING // 2 - 1, kind, local].astype(F32)
                    + sums[part, 1, RING // 2 - 1, kind, local].astype(F32)
                )
                pieces.append(total.reshape(2 * SIDE, CAP, SLICE))
        back[pl.ds(part * 2 * SIDE, 2 * SIDE)] = jnp.concatenate(pieces, axis=1).astype(BF16)
        for half in range(2):
            index = 2 * part + half
            row = lax.rem(y + SIDE - STEPS_Y[index], SIDE) * SIDE

            def send(step, carry):
                dest = row + lax.rem(x + SIDE - step, SIDE)
                pltpu.make_async_remote_copy(
                    src_ref=back.at[index * SIDE + step], dst_ref=returned.at[chip],
                    send_sem=back_send, recv_sem=back_recv,
                    device_id={"expert": dest}, device_id_type=MESH,
                ).start()
                return carry

            lax.fori_loop(1 if index == 0 else 0, SIDE, send, 0)

    def terms(kind, mine):
        half = dp if mine else 1 - dp
        store = keep_half if mine else send_half
        other = pre_grad if kind == 0 else hidden

        def one(step, carry):
            local, q = lax.div(step, RING // 2), lax.rem(step, RING // 2)
            left = jnp.concatenate(
                [rows[part, half * (RING // 2) + q, kind, local] for part in range(PARTS)], axis=0
            )
            span = pl.ds(pl.multiple_of(q * SLICE, SLICE), SLICE)
            store[kind, local, span, :] = contract(left, other[local], 0, 0).astype(BF16)
            return carry

        lax.fori_loop(0, LOCAL * (RING // 2), one, 0)

    term_copy = pltpu.make_async_remote_copy(
        src_ref=send_half, dst_ref=got_terms, send_sem=term_send, recv_sem=term_recv,
        device_id={"dp": 1 - dp}, device_id_type=MESH,
    )
    keep_copy = pltpu.make_async_copy(keep_half, own_terms, keep_sem)

    for part in range(PARTS):
        dispatch(part)
    enter(0)
    enter(1)
    for step in (2, 3, 4):
        forward(0, step)
        forward(1, step)
    enter(2)
    enter(3)
    loads[2].wait()
    experts(0)
    forward(2, 2)
    experts(1)
    forward(3, 2)
    forward(2, 3)
    forward(3, 3)
    forward(2, 4)
    forward(3, 4)
    add(0, 1)
    add(1, 1)
    add(0, 2)
    add(1, 2)
    experts(2)
    add(0, 3)
    experts(3)
    add(1, 3)
    add(0, 4)
    add(1, 4)
    add(2, 1)
    add(3, 1)
    terms(0, False)
    add(2, 2)
    give_back(0)
    add(3, 2)
    terms(1, False)
    term_copy.start()
    give_back(1)
    add(2, 3)
    terms(0, True)
    add(3, 3)
    terms(1, True)
    keep_copy.start()
    add(2, 4)
    add(3, 4)
    give_back(2)
    give_back(3)

    returned[chip] = back[0]
    wait_bytes(returned.at[pl.ds(0, peers - 1)], back_recv)
    out_rows = returned[:, 0:16, :].reshape(slots, SLICE)
    in_rows = returned[:, 16:32, :].reshape(slots, SLICE)
    mixed[...] = (contract(gate_hi[...], out_rows, 0, 0) + contract(gate_lo[...], out_rows, 0, 0)).astype(BF16)
    lat_grad[...] = contract(mask[...], in_rows, 0, 0).astype(BF16)

    term_copy.wait()
    keep_copy.wait()
    wait_bytes(outgoing.at[pl.ds(0, peers - 1)], out_send)
    wait_bytes(back.at[pl.ds(0, peers - 1)], back_send)
    for part in range(PARTS):
        for way in range(2):
            for step in range(1, RING // 2 + 1):
                hop(part, way, step, True).wait_send()
                sum_hop(part, way, step)[1].wait_send()


def shards(latent, grad_out, expert_weights, expert_ids, slot_index, kept, gate_weights):
    tokens, width = latent.shape
    units = expert_weights.shape[3]
    peers = lax.axis_size("expert")
    slots = peers * LOCAL * CAP
    half = width // 2
    vmem = pl.BlockSpec(memory_space=pltpu.VMEM)
    anywhere = pl.BlockSpec(memory_space=pl.ANY)
    dma = pltpu.SemaphoreType.DMA
    ring = (PARTS, 2, RING // 2)
    mixed, lat_grad, own, got = pl.pallas_call(
        block_kernel,
        out_shape=(
            jax.ShapeDtypeStruct((tokens, SLICE), BF16),
            jax.ShapeDtypeStruct((tokens, SLICE), BF16),
            jax.ShapeDtypeStruct((2, LOCAL, half, units), BF16),
            jax.ShapeDtypeStruct((2, LOCAL, half, units), BF16),
        ),
        in_specs=[vmem] * 4 + [anywhere] * 3,
        out_specs=(vmem, vmem, anywhere, anywhere),
        scratch_shapes=[
            pltpu.VMEM((tokens, SLICE), BF16),
            pltpu.VMEM((tokens, SLICE), BF16),
            pltpu.VMEM((2, LOCAL, width, units), BF16),
            pltpu.VMEM((slots, tokens), BF16),
            pltpu.VMEM((slots, tokens), BF16),
            pltpu.VMEM((slots, tokens), BF16),
            pltpu.VMEM((peers, 32, SLICE), BF16),
            pltpu.VMEM((peers, 32, SLICE), BF16),
            pltpu.VMEM((PARTS, RING, 2, LOCAL, ROWS, SLICE), BF16),
            pltpu.VMEM((PARTS, RING, 2, LOCAL, ROWS, SLICE), BF16),
            pltpu.VMEM(ring + (2, LOCAL, ROWS, SLICE), BF16),
            pltpu.VMEM((peers, 32, SLICE), BF16),
            pltpu.VMEM((peers, 32, SLICE), BF16),
            pltpu.VMEM((LOCAL, PARTS * ROWS, units), BF16),
            pltpu.VMEM((LOCAL, PARTS * ROWS, units), BF16),
            pltpu.VMEM((2, LOCAL, half, units), BF16),
            pltpu.VMEM((2, LOCAL, half, units), BF16),
            dma((3,)),
            dma,
            dma((PARTS,)),
            dma(ring),
            dma(ring),
            dma(ring),
            dma(ring),
            dma,
            dma,
            dma,
            dma,
            dma,
        ],
        compiler_params=pltpu.CompilerParams(
            collective_id=0, has_side_effects=True, vmem_limit_bytes=40 * 2**20
        ),
    )(expert_ids.T, slot_index.T, kept.T, gate_weights.T, latent, grad_out, expert_weights)
    return (mixed, lat_grad, own.astype(F32) + got.astype(F32))


def solution(mesh):
    in_specs = (
        P(("dp", "expert"), None),
        P(("dp", "expert"), None),
        P(None, "expert", None, "tensor"),
        P(("dp", "expert"), None),
        P(("dp", "expert"), None),
        P(("dp", "expert"), None),
        P(("dp", "expert"), None),
    )
    out_specs = (
        P(("dp", "expert"), "tensor"),
        P(("dp", "expert"), "tensor"),
        P(None, "expert", "dp", "tensor"),
    )
    return jax.shard_map(shards, mesh=mesh, in_specs=in_specs, out_specs=out_specs, check_vma=False)
```

```python
import jax
import jax.numpy as jnp
from jax import lax
from jax.experimental import pallas as pl
from jax.experimental.pallas import tpu as pltpu
from jax.sharding import PartitionSpec as P

SIDE = 8
RING = 8
STEPS = 3
PARTS = 4
CAP = 8
LOCAL = 2
SLICE = 128
ROWS = 128
STEPS_Y = (0, 4, 1, 7, 2, 6, 3, 5)
MESH = pl.DeviceIdType.MESH
BF16 = jnp.bfloat16
F32 = jnp.float32


def contract(left, right, dim_left, dim_right):
    return lax.dot_general(
        left, right, (((dim_left,), (dim_right,)), ((), ())), preferred_element_type=F32
    )


def block_kernel(
    ids_hbm, slot_hbm, kept_hbm, gate_hbm, lat_hbm, grad_hbm, w_hbm,
    mixed, lat_grad, own_terms, got_terms,
    ids, slot, kept, gate, lat, grad, w, mask, gate_hi, gate_lo,
    outgoing, incoming, rows, partial, sums, back, returned, far_send, far_got, hidden, pre_grad, keep_half, send_half,
    load_sem, out_send, out_recv, gather_send, gather_recv, sum_send, sum_recv,
    back_send, back_recv, far_sems, term_send, term_recv, keep_sem, row_here,
):
    dp = lax.axis_index("dp")
    chip = lax.axis_index("expert")
    z = lax.axis_index("tensor")
    y, x = lax.div(chip, SIDE), lax.rem(chip, SIDE)
    peers = SIDE * SIDE
    slots = peers * LOCAL * CAP
    above, below = lax.rem(z + 1, RING), lax.rem(z + RING - 1, RING)

    across = lax.rem(z + RING // 2, RING)
    span = pl.ds(pl.multiple_of(z * SLICE, SLICE), SLICE)
    far_span = pl.ds(pl.multiple_of(across * SLICE, SLICE), SLICE)
    barrier = pltpu.get_barrier_semaphore()

    def greet(step, carry):
        pl.semaphore_signal(
            barrier, inc=1, device_id={"expert": y * SIDE + lax.rem(x + step, SIDE)}, device_id_type=MESH
        )
        pl.semaphore_signal(
            barrier, inc=1, device_id={"expert": lax.rem(y + step, SIDE) * SIDE + x}, device_id_type=MESH
        )
        return carry

    def vouch(step, carry):
        pl.semaphore_signal(
            row_here, inc=1, device_id={"expert": lax.rem(y + step, SIDE) * SIDE + x}, device_id_type=MESH
        )
        return carry

    lax.fori_loop(1, SIDE, greet, 0)
    for position in (above, below, across):
        pl.semaphore_signal(barrier, inc=1, device_id={"tensor": position}, device_id_type=MESH)
    pl.semaphore_signal(barrier, inc=1, device_id={"dp": 1 - dp}, device_id_type=MESH)

    loads = [
        pltpu.make_async_copy(ids_hbm, ids, load_sem.at[0]),
        pltpu.make_async_copy(slot_hbm, slot, load_sem.at[1]),
        pltpu.make_async_copy(kept_hbm, kept, load_sem.at[2]),
        pltpu.make_async_copy(gate_hbm, gate, load_sem.at[3]),
        pltpu.make_async_copy(lat_hbm.at[:, span], lat.at[0], load_sem.at[4]),
        pltpu.make_async_copy(grad_hbm.at[:, span], grad.at[0], load_sem.at[5]),
        pltpu.make_async_copy(lat_hbm.at[:, far_span], lat.at[1], load_sem.at[7]),
        pltpu.make_async_copy(grad_hbm.at[:, far_span], grad.at[1], load_sem.at[8]),
        pltpu.make_async_copy(w_hbm, w, load_sem.at[6]),
    ]
    for load in loads:
        load.start()
    pl.semaphore_wait(barrier, 2 * (SIDE - 1) + 4)
    lax.fori_loop(1, SIDE, vouch, 0)

    for load in loads[:8]:
        load.wait()
    target = jnp.where(kept[...] > 0, ids[...] * CAP + slot[...], slots)
    gates = gate[...]

    def build(ahead, carry):
        step = lax.rem(y + ahead, SIDE)
        begin = pl.multiple_of(step * 128, 128)
        slot_of = begin + lax.broadcasted_iota(jnp.int32, (128, 128), 0)
        placed = jnp.zeros((128, 128), F32)
        weight = jnp.zeros((128, 128), F32)
        for k in range(ids.shape[0]):
            same = target[k : k + 1, :] == slot_of
            placed = jnp.where(same, 1.0, placed)
            weight = jnp.where(same, gates[k : k + 1, :], weight)
        hi = weight.astype(BF16)
        here = pl.ds(begin, 128)
        mask[here, :] = placed.astype(BF16)
        gate_hi[here, :] = hi
        gate_lo[here, :] = (weight - hi.astype(F32)).astype(BF16)
        onehot = placed.astype(BF16)
        scale = jnp.sum(weight, axis=1, keepdims=True)
        dests = pl.ds(pl.multiple_of(step * 8, 8), 8)
        for far in range(2):
            lat_rows = contract(onehot, lat[far], 1, 0).astype(BF16)
            grad_rows = (scale * contract(onehot, grad[far], 1, 0)).astype(BF16)
            first = 2 * 16 * far
            outgoing[dests, first : first + 16, :] = lat_rows.reshape(8, 16, SLICE)
            outgoing[dests, first + 16 : first + 32, :] = grad_rows.reshape(8, 16, SLICE)
        return carry

    spans = (pl.ds(0, 32), pl.ds(32, 32))

    def dispatch_row(index, far):
        row = lax.rem(y + STEPS_Y[index], SIDE) * SIDE

        def send(step, carry):
            dest = row + lax.rem(x + step, SIDE)
            pltpu.make_async_remote_copy(
                src_ref=outgoing.at[dest, spans[far]], dst_ref=incoming.at[index * SIDE + step, spans[far]],
                send_sem=out_send.at[far], recv_sem=out_recv.at[far, index // 2],
                device_id={"expert": dest}, device_id_type=MESH,
            ).start()
            return carry

        lax.fori_loop(1 if index == 0 else 0, SIDE, send, 0)

    def dispatch(part, far):
        dispatch_row(2 * part, far)
        dispatch_row(2 * part + 1, far)

    def wait_bytes(ref, sem):
        pltpu.make_async_copy(ref, ref, sem).wait()

    def hop(part, way, kind):
        to, ahead = (above, 1) if way == 0 else (below, RING - 1)
        owner = lax.rem(z + (0, RING - ahead, RING // 2)[kind], RING)
        return pltpu.make_async_remote_copy(
            src_ref=rows.at[part, owner], dst_ref=rows.at[part, owner],
            send_sem=gather_send.at[part, way, kind], recv_sem=gather_recv.at[part, way, kind],
            device_id={"tensor": to}, device_id_type=MESH,
        )

    def landed(part, way, kind):
        behind = RING - 1 if way == 0 else 1
        owner = lax.rem(z + behind + (0, behind, RING // 2)[kind], RING)
        wait_bytes(rows.at[part, owner], gather_recv.at[part, way, kind])

    def unpack(part, far):
        first = part * 2 * SIDE
        if part == 0:
            incoming[0, spans[far]] = outgoing[chip, spans[far]]
            wait_bytes(incoming.at[pl.ds(1, 2 * SIDE - 1), spans[far]], out_recv.at[far, part])
        else:
            wait_bytes(incoming.at[pl.ds(first, 2 * SIDE), spans[far]], out_recv.at[far, part])
        got = incoming[pl.ds(first, 2 * SIDE), spans[far], :].astype(F32).reshape(2 * SIDE, 4, CAP, SLICE)
        for kind in range(2):
            for local in range(LOCAL):
                rows[part, across if far else z, kind, local] = (
                    got[:, 2 * kind + local].reshape(ROWS, SLICE).astype(BF16)
                )

    def enter(part, far):
        unpack(part, far)
        for way in range(2):
            hop(part, way, 2 if far else 0).start()

    def forward(part):
        for way in range(2):
            landed(part, way, 0)
            hop(part, way, 1).start()

    def experts(part):
        for way in range(2):
            landed(part, way, 1)
            landed(part, way, 2)

        def one(local, carry):
            got_in = jnp.concatenate([rows[part, q, 0, local] for q in range(RING)], axis=1)
            got_grad = jnp.concatenate([rows[part, q, 1, local] for q in range(RING)], axis=1)
            active = jnp.maximum(contract(got_in, w[0, local], 1, 0), 0.0)
            unit = (active * active).astype(BF16)
            unit_grad = (contract(got_grad, w[1, local], 1, 0) * 2.0 * active).astype(BF16)
            here = pl.ds(part * ROWS, ROWS)
            hidden[local, here, :] = unit
            pre_grad[local, here, :] = unit_grad
            for q in range(0, RING, 2):
                cols = pl.ds(q * SLICE, 2 * SLICE)
                out_cols = contract(unit, w[1, local, cols, :], 1, 1).astype(BF16)
                in_cols = contract(unit_grad, w[0, local, cols, :], 1, 1).astype(BF16)
                for side in range(2):
                    span = slice(side * SLICE, (side + 1) * SLICE)
                    partial[part, q + side, 0, local] = out_cols[:, span]
                    partial[part, q + side, 1, local] = in_cols[:, span]
            return carry

        lax.fori_loop(0, LOCAL, one, 0)

    def sum_hop(part, way, kind):
        to, ahead = (above, 1) if way == 0 else (below, RING - 1)
        owner = lax.rem(z + ahead * (2, 1, RING // 2 + 1)[kind], RING)
        return owner, pltpu.make_async_remote_copy(
            src_ref=partial.at[part, owner], dst_ref=sums.at[part, way, kind],
            send_sem=sum_send.at[part, way, kind], recv_sem=sum_recv.at[part, way, kind],
            device_id={"tensor": to}, device_id_type=MESH,
        )

    def start_sums(part):
        for kind in (0, 2):
            for way in range(2):
                sum_hop(part, way, kind)[1].start()

    def add(part):
        for way in range(2):
            owner, copy = sum_hop(part, way, 1)
            wait_bytes(sums.at[part, way, 0], sum_recv.at[part, way, 0])
            for kind in range(2):
                for local in range(LOCAL):
                    partial[part, owner, kind, local] = (
                        partial[part, owner, kind, local].astype(F32)
                        + sums[part, way, 0, kind, local].astype(F32)
                    ).astype(BF16)
            copy.start()

    def give_back(part, far):
        pieces = []
        last = 2 if far else 1
        for way in range(2):
            wait_bytes(sums.at[part, way, last], sum_recv.at[part, way, last])
        for kind in range(2):
            for local in range(LOCAL):
                total = partial[part, across if far else z, kind, local].astype(F32)
                for way in range(2):
                    total += sums[part, way, last, kind, local].astype(F32)
                pieces.append(total.reshape(2 * SIDE, CAP, SLICE))
        back[far, pl.ds(part * 2 * SIDE, 2 * SIDE)] = jnp.concatenate(pieces, axis=1).astype(BF16)
        for half in range(2):
            index = 2 * part + half
            row = lax.rem(y + SIDE - STEPS_Y[index], SIDE) * SIDE

            def send(step, carry):
                dest = row + lax.rem(x + SIDE - step, SIDE)
                pltpu.make_async_remote_copy(
                    src_ref=back.at[far, index * SIDE + step], dst_ref=returned.at[far, chip],
                    send_sem=back_send.at[far], recv_sem=back_recv.at[far, part],
                    device_id={"expert": dest}, device_id_type=MESH,
                ).start()
                return carry

            lax.fori_loop(1 if index == 0 else 0, SIDE, send, 0)

    def combine(far):
        out = jnp.zeros((gate_hi.shape[1], SLICE), F32)
        in_grad = jnp.zeros((gate_hi.shape[1], SLICE), F32)
        returned[far, chip] = back[far, 0]
        for index in range(SIDE):
            if index % 2 == 0:
                wait_bytes(returned.at[far, pl.ds(0, 2 * SIDE - (index == 0))], back_recv.at[far, index // 2])
            row = lax.rem(y + STEPS_Y[index], SIDE)
            got = returned[far, pl.ds(row * SIDE, SIDE)]
            out_rows = got[:, 0:16].reshape(SIDE * 16, SLICE)
            in_rows = got[:, 16:32].reshape(SIDE * 16, SLICE)
            here = pl.ds(pl.multiple_of(row * SIDE * 16, SIDE * 16), SIDE * 16)
            out += contract(gate_hi[here, :], out_rows, 0, 0) + contract(gate_lo[here, :], out_rows, 0, 0)
            in_grad += contract(mask[here, :], in_rows, 0, 0)
        return out, in_grad

    def terms(kind, mine):
        half = dp if mine else 1 - dp
        store = keep_half if mine else send_half
        other = pre_grad if kind == 0 else hidden

        def one(step, carry):
            local, q = lax.div(step, RING // 2), lax.rem(step, RING // 2)
            left = jnp.concatenate(
                [rows[part, half * (RING // 2) + q, kind, local] for part in range(PARTS)], axis=0
            )
            span = pl.ds(pl.multiple_of(q * SLICE, SLICE), SLICE)
            store[kind, local, span, :] = contract(left, other[local], 0, 0).astype(BF16)
            return carry

        lax.fori_loop(0, LOCAL * (RING // 2), one, 0)

    term_copy = pltpu.make_async_remote_copy(
        src_ref=send_half, dst_ref=got_terms, send_sem=term_send, recv_sem=term_recv,
        device_id={"dp": 1 - dp}, device_id_type=MESH,
    )
    keep_copy = pltpu.make_async_copy(keep_half, own_terms, keep_sem)

    far_copy = pltpu.make_async_remote_copy(
        src_ref=far_send, dst_ref=far_got, send_sem=far_sems.at[0], recv_sem=far_sems.at[1],
        device_id={"tensor": across}, device_id_type=MESH,
    )

    build(STEPS_Y[0], 0)
    dispatch_row(0, 0)
    build(STEPS_Y[1], 0)
    pl.semaphore_wait(row_here, SIDE - 1)
    dispatch_row(1, 0)
    lax.fori_loop(1, 4, build, 0)
    lax.fori_loop(5, SIDE, build, 0)
    dispatch(1, 0)
    enter(0, 0)
    dispatch(2, 0)
    enter(1, 0)
    dispatch(3, 0)
    enter(2, 0)
    dispatch(0, 1)
    enter(3, 0)
    dispatch(1, 1)
    forward(0)
    dispatch(2, 1)
    forward(1)
    dispatch(3, 1)
    forward(2)
    forward(3)
    for part in range(PARTS):
        enter(part, 1)
    loads[8].wait()
    for part in range(PARTS):
        experts(part)
        start_sums(part)
    for part in range(PARTS):
        add(part)
        give_back(part, 1)
    terms(0, False)
    terms(1, False)
    term_copy.start()
    give_back(0, 0)
    terms(0, True)
    give_back(1, 0)
    terms(1, True)
    keep_copy.start()
    far_out, far_in = combine(1)
    far_send[0] = far_out.astype(BF16)
    far_send[1] = far_in.astype(BF16)
    give_back(2, 0)
    give_back(3, 0)
    far_copy.start()
    out, in_grad = combine(0)
    far_copy.wait_recv()
    mixed[...] = (out + far_got[0].astype(F32)).astype(BF16)
    lat_grad[...] = (in_grad + far_got[1].astype(F32)).astype(BF16)

    term_copy.wait()
    keep_copy.wait()
    far_copy.wait_send()
    for far in range(2):
        wait_bytes(outgoing.at[pl.ds(0, peers - 1), spans[far]], out_send.at[far])
        wait_bytes(back.at[far, pl.ds(0, peers - 1)], back_send.at[far])
    for part in range(PARTS):
        for way in range(2):
            for kind in range(STEPS):
                hop(part, way, kind).wait_send()
                sum_hop(part, way, kind)[1].wait_send()


def shards(latent, grad_out, expert_weights, expert_ids, slot_index, kept, gate_weights):
    tokens, width = latent.shape
    units = expert_weights.shape[3]
    topk = expert_ids.shape[1]
    peers = lax.axis_size("expert")
    slots = peers * LOCAL * CAP
    half = width // 2
    vmem = pl.BlockSpec(memory_space=pltpu.VMEM)
    anywhere = pl.BlockSpec(memory_space=pl.ANY)
    hbm = pl.BlockSpec(memory_space=pltpu.HBM)
    dma = pltpu.SemaphoreType.DMA
    ring = (PARTS, 2, STEPS)
    mixed, lat_grad, own, got = pl.pallas_call(
        block_kernel,
        out_shape=(
            jax.ShapeDtypeStruct((tokens, SLICE), BF16),
            jax.ShapeDtypeStruct((tokens, SLICE), BF16),
            jax.ShapeDtypeStruct((2, LOCAL, half, units), BF16),
            jax.ShapeDtypeStruct((2, LOCAL, half, units), BF16),
        ),
        in_specs=[hbm] * 7,
        out_specs=(vmem, vmem, anywhere, anywhere),
        scratch_shapes=[
            pltpu.VMEM((topk, tokens), jnp.int32),
            pltpu.VMEM((topk, tokens), jnp.int32),
            pltpu.VMEM((topk, tokens), jnp.int32),
            pltpu.VMEM((topk, tokens), F32),
            pltpu.VMEM((2, tokens, SLICE), BF16),
            pltpu.VMEM((2, tokens, SLICE), BF16),
            pltpu.VMEM((2, LOCAL, width, units), BF16),
            pltpu.VMEM((slots, tokens), BF16),
            pltpu.VMEM((slots, tokens), BF16),
            pltpu.VMEM((slots, tokens), BF16),
            pltpu.VMEM((peers, 64, SLICE), BF16),
            pltpu.VMEM((peers, 64, SLICE), BF16),
            pltpu.VMEM((PARTS, RING, 2, LOCAL, ROWS, SLICE), BF16),
            pltpu.VMEM((PARTS, RING, 2, LOCAL, ROWS, SLICE), BF16),
            pltpu.VMEM(ring + (2, LOCAL, ROWS, SLICE), BF16),
            pltpu.VMEM((2, peers, 32, SLICE), BF16),
            pltpu.VMEM((2, peers, 32, SLICE), BF16),
            pltpu.VMEM((2, tokens, SLICE), BF16),
            pltpu.VMEM((2, tokens, SLICE), BF16),
            pltpu.VMEM((LOCAL, PARTS * ROWS, units), BF16),
            pltpu.VMEM((LOCAL, PARTS * ROWS, units), BF16),
            pltpu.VMEM((2, LOCAL, half, units), BF16),
            pltpu.VMEM((2, LOCAL, half, units), BF16),
            dma((9,)),
            dma((2,)),
            dma((2, PARTS)),
            dma(ring),
            dma(ring),
            dma(ring),
            dma(ring),
            dma((2,)),
            dma((2, PARTS)),
            dma((2,)),
            dma,
            dma,
            dma,
            pltpu.SemaphoreType.REGULAR,
        ],
        compiler_params=pltpu.CompilerParams(
            collective_id=0, has_side_effects=True, vmem_limit_bytes=60 * 2**20
        ),
    )(expert_ids.T, slot_index.T, kept.T, gate_weights.T, latent, grad_out, expert_weights)
    return (mixed, lat_grad, own.astype(F32) + got.astype(F32))


def solution(mesh):
    in_specs = (
        P(("dp", "expert"), None),
        P(("dp", "expert"), None),
        P(None, "expert", None, "tensor"),
        P(("dp", "expert"), None),
        P(("dp", "expert"), None),
        P(("dp", "expert"), None),
        P(("dp", "expert"), None),
    )
    out_specs = (
        P(("dp", "expert"), "tensor"),
        P(("dp", "expert"), "tensor"),
        P(None, "expert", "dp", "tensor"),
    )
    return jax.shard_map(shards, mesh=mesh, in_specs=in_specs, out_specs=out_specs, check_vma=False)
```
